512 devices in a mesh: expert: 8 (over z_lo, core), ffn: 16 (over y, z_hi), section: 4 (over x).
Axes of the slice: x: 4, y: 4, z: 16 (z_hi: 4, z_lo: 4; z = z_hi * 4 + z_lo), core: 2. Of those that a mesh axis runs over, the one named last changes fastest.
Arguments:
- layer_input: bfloat16 [1024, 6144], P('expert', 'section'), may hold values from -6 to 6
- out_grad: bfloat16 [1024, 6144], P('expert', 'section'), may hold values from -6 to 6
- scores: bfloat16 [8, 384], P(None, 'expert'), may hold values from 0.049804688 to 1
- picks: int32 [8, 384], P(None, 'expert'), may hold values from 0 to 127, as said below
- w_gate: bfloat16 [8, 6144, 6144], P('expert', 'ffn', 'section'), may hold values from -0.078125 to 0.078125
- w_up: bfloat16 [8, 6144, 6144], P('expert', 'ffn', 'section'), may hold values from -0.078125 to 0.078125
- w_down: bfloat16 [8, 6144, 6144], P('expert', 'ffn', 'section'), may hold values from -0.078125 to 0.078125
Outputs:
- input_grad: bfloat16 [1024, 6144], P('expert', 'section')
- score_grad: bfloat16 [8, 384], P(None, 'expert')
The draws below stay inside these ranges and needn't reach their ends.
Inputs may be any that keep to these rules, and one draw needn't show every extreme that they name: `picks`: in each row, the columns j * 48 to (j + 1) * 48 - 1 hold 48 different indices of tokens of the j-th shard of 128 tokens.
All inputs are finite; a program needn't handle non-finite values.
Results may differ from the reference program's by a relative error of at most 0.0057.
Values may be sent and summed in bfloat16 or wider, within the bound.
No kernel may reach another device: no remote copies, remote signals or barrier semaphores. Data moves between devices by JAX's collectives and lax.ppermute only.
A program may use at most 64 MiB of HBM per device.

```python
import math
import jax
import jax.numpy as jnp

D = 6144
TOK_DEV = 128
PICK = 48
EXPERTS = 8
FF = 6144
CAP = 384
TOKENS = 1024
N_EXPERT = 8


def draw_picks(key, part):
    key = jax.random.fold_in(key, 7)
    noise = jax.random.randint(key, (EXPERTS, N_EXPERT, TOK_DEV), 0, 1 << 20)
    ranked = noise * TOK_DEV + jnp.arange(TOK_DEV, dtype=jnp.int32)[None, None, :]
    order = jnp.argsort(ranked, axis=-1, stable=True).astype(jnp.int32)
    return order[:, :, :PICK].reshape(EXPERTS, CAP).astype(jnp.int32)


def block_scale(own_key, extent, pieces, smallest, largest):
    def one(axis_at, shards_of):
        draws = jax.random.uniform(jax.random.fold_in(jax.random.fold_in(own_key, 6), axis_at), (shards_of,), jnp.float32, smallest / len(pieces), largest / len(pieces))
        return jnp.repeat(jnp.exp(draws), extent[axis_at] // shards_of).reshape((-1,) + (1,) * (len(extent) - axis_at - 1))

    factor_of = one(*pieces[0])
    for cut in pieces[1:]:
        factor_of = factor_of * one(*cut)
    return factor_of


def scatter_about(rng, dims, spread, most, shards=(), held_as=jnp.bfloat16):
    entries = spread * jax.random.normal(rng, dims, jnp.float32)
    if shards:
        entries = entries * block_scale(rng, dims, shards, -0.22, 0.18)
    return jnp.clip(entries, -most, most).astype(held_as)


def setup_inputs(seed: int = 0) -> dict:
    streams_of = jax.random.split(jax.random.key(seed), 8)
    return {
        "layer_input": scatter_about(streams_of[0], (TOKENS, D), 1.0, 6.0, ((0, 8), (1, 4))),
        "out_grad": scatter_about(streams_of[1], (TOKENS, D), 1.0, 6.0, ((0, 8), (1, 4))),
        "scores": jnp.clip(jnp.exp(math.log(1.0) - 2.9996462 * jax.random.uniform(streams_of[2], (EXPERTS, CAP), jnp.float32) ** block_scale(streams_of[2], (EXPERTS, CAP), ((1, 8),), -0.2, 0.2)), 0.049804688, 1.0).astype(jnp.bfloat16),
        "picks": draw_picks(jax.random.fold_in(streams_of[7], 71), 0),
        "w_gate": scatter_about(streams_of[4], (EXPERTS, FF, D), D ** -0.5, 0.078125, ((0, 8), (1, 16), (2, 4))),
        "w_up": scatter_about(streams_of[5], (EXPERTS, FF, D), D ** -0.5, 0.078125, ((0, 8), (1, 16), (2, 4))),
        "w_down": scatter_about(streams_of[6], (EXPERTS, FF, D), FF ** -0.5, 0.078125, ((0, 8), (1, 16), (2, 4))),
    }


def reference(layer_input, out_grad, scores, picks, w_gate, w_up, w_down):
    column = jnp.arange(CAP, dtype=jnp.int32)
    source = (column // PICK).astype(jnp.int32)
    grad_total = jnp.zeros((TOKENS, D), jnp.float32)
    score_rows = []
    for expert in range(EXPERTS):
        rows = (source * TOK_DEV + picks[expert]).astype(jnp.int32)
        x_rows = layer_input[rows]
        g_rows = out_grad[rows]
        gate = jnp.dot(x_rows, w_gate[expert].T, preferred_element_type=jnp.float32)
        up = jnp.dot(x_rows, w_up[expert].T, preferred_element_type=jnp.float32)
        back = jnp.dot(g_rows, w_down[expert].T, preferred_element_type=jnp.float32)
        weight = scores[expert].astype(jnp.float32)[:, None]
        sig = jax.nn.sigmoid(gate)
        act = gate * sig
        hid = act * up
        score_rows.append(jnp.sum(hid * back, axis=1).astype(jnp.bfloat16))
        grad_h = weight * back
        d_up = (grad_h * act).astype(jnp.bfloat16)
        d_gate = (grad_h * up * sig * (1.0 + gate * (1.0 - sig))).astype(jnp.bfloat16)
        row_grad = jnp.dot(d_gate, w_gate[expert], preferred_element_type=jnp.float32) + jnp.dot(d_up, w_up[expert], preferred_element_type=jnp.float32)
        row_grad = row_grad.astype(jnp.bfloat16).astype(jnp.float32)
        grad_total = grad_total.at[rows].add(row_grad)
    return grad_total.astype(jnp.bfloat16), jnp.stack(score_rows, axis=0)
```

```python
import functools

import jax
import jax.numpy as jnp
from jax import lax
from jax.experimental import pallas as pl
from jax.experimental.pallas import tpu as pltpu
from jax.sharding import Mesh, PartitionSpec as P

BF16 = jnp.bfloat16
F32 = jnp.float32
LANES = 128
PAD = 16
EXPERT = ("zl", "c")
VMEM = pl.BlockSpec(memory_space=pltpu.VMEM)
SMEM = pl.BlockSpec(memory_space=pltpu.SMEM)


def dot(a, b, ca, cb):
    return lax.dot_general(a, b, (((ca,), (cb,)), ((), ())), preferred_element_type=F32)


def call(kernel, out_shape, flops, *args, specs=None):
    nbytes = sum(a.size * a.dtype.itemsize for a in args)
    nbytes += out_shape.size * out_shape.dtype.itemsize
    return pl.pallas_call(
        kernel,
        out_shape=out_shape,
        in_specs=specs or [VMEM] * len(args),
        out_specs=VMEM,
        compiler_params=pltpu.CompilerParams(vmem_limit_bytes=40 << 20),
        cost_estimate=pl.CostEstimate(flops=flops, bytes_accessed=nbytes, transcendentals=0),
    )(*args)


def placed(picks_ref, e, tokens):
    row = picks_ref[pl.ds(e, 1), :]
    at = lax.broadcasted_iota(jnp.int32, (tokens, row.shape[1]), 0)
    return (at == row).astype(BF16)


def pick_kernel(y_ref, picks_ref, x_ref, g_ref, out_ref):
    experts, tokens = picks_ref.shape[0], x_ref.shape[0]
    share = out_ref.shape[2] // 2
    cols = pl.ds(pl.multiple_of(y_ref[0] * share, LANES), share)
    x, g = x_ref[:, cols], g_ref[:, cols]
    for e in range(experts):
        hot = placed(picks_ref, e, tokens)
        out_ref[e, :, :share] = dot(hot, x, 0, 0).astype(BF16)
        out_ref[e, :, share:] = dot(hot, g, 0, 0).astype(BF16)


def forward_kernel(xg_ref, gate_ref, up_ref, down_ref, out_ref):
    parts, _, both = xg_ref.shape
    share = both // 2
    hidden = gate_ref.shape[0]
    for i, (w_ref, at) in enumerate(((gate_ref, 0), (up_ref, 0), (down_ref, share))):
        total = None
        for k in range(parts):
            term = dot(xg_ref[k, :, at : at + share], w_ref[:, k * share : (k + 1) * share], 1, 1)
            total = term if total is None else total + term
        out_ref[:, i * hidden : (i + 1) * hidden] = total.astype(BF16)


def middle_kernel(part_ref, score_ref, out_ref):
    hidden = part_ref.shape[2] // 3

    def total(i):
        pieces = [part_ref[k, :, i * hidden : (i + 1) * hidden].astype(F32) for k in range(part_ref.shape[0])]
        return functools.reduce(lambda a, b: a + b, pieces)

    gate, up, back = total(0), total(1), total(2)
    sig = 1.0 / (1.0 + jnp.exp(-gate))
    act = gate * sig
    score = jnp.sum(act * up * back, axis=1, keepdims=True)
    grad_h = score_ref[...] * back
    out_ref[:, :hidden] = (grad_h * up * sig * (1.0 + gate * (1.0 - sig))).astype(BF16)
    out_ref[:, hidden : 2 * hidden] = (grad_h * act).astype(BF16)
    high = score.astype(BF16).astype(F32)
    lane = lax.broadcasted_iota(jnp.int32, (score.shape[0], LANES), 1)
    out_ref[:, 2 * hidden :] = jnp.where(lane == 0, high, jnp.where(lane == 1, score - high, 0.0)).astype(BF16)


def backward_kernel(d_ref, gate_ref, up_ref, out_ref):
    parts, _, share = out_ref.shape
    rows, hidden = d_ref.shape[0], gate_ref.shape[0]
    d_gate, d_up = d_ref[:, :hidden], d_ref[:, hidden : 2 * hidden]
    pick = (
        lax.broadcasted_iota(jnp.int32, (PAD, LANES), 0) == lax.broadcasted_iota(jnp.int32, (PAD, LANES), 1)
    ).astype(BF16)
    scores = dot(pick, d_ref[:, 2 * hidden :], 1, 1).astype(BF16)
    for k in range(parts):
        cols = slice(k * share, (k + 1) * share)
        total = dot(d_gate, gate_ref[:, cols], 1, 0) + dot(d_up, up_ref[:, cols], 1, 0)
        out_ref[k, :rows, :] = total.astype(BF16)
        out_ref[k, rows:, :] = scores


def scatter_kernel(picks_ref, rows_ref, out_ref):
    total = None
    for e in range(rows_ref.shape[0]):
        term = dot(placed(picks_ref, e, out_ref.shape[0]), rows_ref[e], 1, 0)
        total = term if total is None else total + term
    out_ref[...] = total.astype(BF16)


def exchange(a, axes):
    return lax.all_to_all(a, axes, split_axis=0, concat_axis=0, tiled=True)


def spread(a, axes, n):
    return exchange(jnp.broadcast_to(a[None], (n,) + a.shape), axes)


def local(sizes, layer_input, out_grad, scores, picks, w_gate, w_up, w_down):
    experts, taken = picks.shape
    tokens, width = layer_input.shape
    w_gate, w_up, w_down = w_gate[0], w_up[0], w_down[0]
    hidden = w_gate.shape[0]
    rows = experts * taken
    ny, nx, nh = sizes["y"], sizes["x"], sizes["zh"]
    share, block = width // ny, rows // nx

    y = lax.axis_index("y").astype(jnp.int32).reshape(1)
    sent = call(
        pick_kernel,
        jax.ShapeDtypeStruct((experts, taken, 2 * share), BF16),
        2 * rows * tokens * 2 * share,
        y, picks, layer_input, out_grad,
        specs=[SMEM, VMEM, VMEM, VMEM],
    )
    got = exchange(sent, EXPERT).reshape(rows, 2 * share)
    weight = exchange(scores.reshape(experts, 1, taken), EXPERT).reshape(rows)
    weight = lax.dynamic_slice(weight, (lax.axis_index("x") * block,), (block,))
    weight = weight.astype(F32).reshape(block, 1)
    xg = spread(got, "y", ny)
    part = call(
        forward_kernel,
        jax.ShapeDtypeStruct((rows, 3 * hidden), BF16),
        2 * rows * hidden * width * 3,
        xg, w_gate, w_up, w_down,
    )
    part = exchange(part.reshape(nx, block, 3 * hidden), "x")
    d_block = call(
        middle_kernel,
        jax.ShapeDtypeStruct((block, 2 * hidden + LANES), BF16),
        30 * block * hidden,
        part, weight,
    )
    d = spread(d_block, "x", nx).reshape(rows, 2 * hidden + LANES)
    part = call(
        backward_kernel,
        jax.ShapeDtypeStruct((ny, rows + PAD, share), BF16),
        4 * rows * hidden * width,
        d, w_gate, w_up,
    )
    part = exchange(part, "y")
    summed = jnp.sum(part.astype(F32), axis=0)
    row_part = summed[:rows].astype(BF16).reshape(experts, taken, share)
    score_part = (summed[rows] + summed[rows + 1]).reshape(experts, taken)
    high = score_part.astype(BF16)
    low = (score_part - high.astype(F32)).astype(BF16)
    score_part = jnp.stack([high, low], axis=1)
    score_all = exchange(
        jnp.broadcast_to(score_part[None], (nh,) + score_part.shape).reshape(nh * experts, 2, taken),
        ("zh",) + EXPERT,
    )
    score_grad = score_all.reshape(nh, experts, 2, taken).astype(F32).sum(axis=(0, 2)).astype(BF16)
    back = exchange(row_part, EXPERT)
    token_part = call(
        scatter_kernel,
        jax.ShapeDtypeStruct((tokens, share), BF16),
        2 * rows * tokens * share,
        picks, back,
    )
    token_grad = jnp.sum(spread(token_part, "zh", nh).astype(F32), axis=0).astype(BF16)
    input_grad = lax.all_gather(token_grad, "y", axis=1, tiled=True)
    return input_grad, score_grad


def solution(mesh):
    sizes = {"zl": 4, "c": 2, "y": 4, "zh": 4, "x": 4}
    fine = Mesh(mesh.devices.reshape(tuple(sizes.values())), tuple(sizes))
    ffn = ("y", "zh")
    placed_in = (
        P(EXPERT, "x"),
        P(EXPERT, "x"),
        P(None, EXPERT),
        P(None, EXPERT),
        P(EXPERT, ffn, "x"),
        P(EXPERT, ffn, "x"),
        P(EXPERT, ffn, "x"),
    )
    return jax.shard_map(
        functools.partial(local, sizes),
        mesh=fine,
        in_specs=placed_in,
        out_specs=(P(EXPERT, "x"), P(None, EXPERT)),
        check_vma=False,
    )
```

```python
import functools

import jax
import jax.numpy as jnp
from jax import lax
from jax.experimental import pallas as pl
from jax.experimental.pallas import tpu as pltpu
from jax.sharding import Mesh, PartitionSpec as P

BF16 = jnp.bfloat16
F32 = jnp.float32
LANES = 128
PAD = 16
EXPERT = ("zl", "c")
RING = ("zl", "c", "zh")
SIZES = {"zl": 4, "c": 2, "y": 4, "zh": 4, "x": 4}
LIMIT = 16
VMEM = pl.BlockSpec(memory_space=pltpu.VMEM)
SMEM = pl.BlockSpec(memory_space=pltpu.SMEM)


def dot(a, b, ca, cb):
    return lax.dot_general(a, b, (((ca,), (cb,)), ((), ())), preferred_element_type=F32)


def iota(shape, axis):
    return lax.broadcasted_iota(jnp.int32, shape, axis)


def sds(shape, dtype=BF16):
    return jax.ShapeDtypeStruct(shape, dtype)


def add_up(pieces):
    return functools.reduce(lambda a, b: a + b, pieces)


def call(kernel, outs, args, *, flops, specs=None, scratch=(), limit=LIMIT):
    nbytes = sum(a.size * a.dtype.itemsize for a in list(args) + jax.tree.leaves(outs))
    return pl.pallas_call(
        kernel,
        out_shape=outs,
        in_specs=specs or [VMEM] * len(args),
        out_specs=jax.tree.map(lambda o: VMEM, outs),
        scratch_shapes=scratch,
        compiler_params=pltpu.CompilerParams(vmem_limit_bytes=limit << 20),
        cost_estimate=pl.CostEstimate(flops=flops, bytes_accessed=nbytes, transcendentals=0),
    )(*args)


BLOCKS = ((0, 0), (0, 1), (1, 0), (-1, 0), (2, 0), (1, 1), (-1, 1), (2, 1))


def at(pos_ref, dz, dc):
    chips, cores = SIZES["zl"], SIZES["c"]
    return lax.rem(pos_ref[0] + (dz + chips), chips) * cores + lax.rem(pos_ref[1] + dc, cores)


def pick_kernel(pos_ref, picks_ref, xg_ref, own_ref, swap_ref, up_ref, down_ref, far_x_ref, far_g_ref, hot_ref):
    experts, taken = picks_ref.shape
    tokens, width = xg_ref.shape[1:]
    row = iota(picks_ref.shape, 0)
    taken_here = picks_ref[...].astype(F32)
    picked = [
        jnp.sum(jnp.where(row == at(pos_ref, *b), taken_here, 0.0), axis=0, keepdims=True) for b in BLOCKS
    ]
    picks = jnp.transpose(jnp.concatenate(picked, axis=0))
    lane = iota((taken, tokens), 1).astype(F32)
    for i in range(experts):
        hot_ref[i * taken : (i + 1) * taken, :] = (lane == picks[:, i : i + 1]).astype(BF16)
    step = 4 * LANES
    for which, far_ref in enumerate((far_x_ref, far_g_ref)):
        for start in range(0, width, step):
            cols = slice(start, start + step)
            rows = dot(hot_ref[...], xg_ref[which, :, cols], 1, 0).astype(BF16)
            blocks = [rows[i * taken : (i + 1) * taken] for i in range(experts)]
            own_ref[which, :, cols] = blocks[0]
            swap_ref[which, :, cols] = blocks[1]
            for dc in range(2):
                up_ref[dc, which, :, cols] = blocks[2 + 3 * dc]
                down_ref[dc, which, :, cols] = blocks[3 + 3 * dc]
                far_ref[dc, :, cols] = blocks[4 + 3 * dc]


def pass_kernel(up_ref, down_ref, far_x_ref, far_g_ref, out_ref):
    out_ref[0] = up_ref[1]
    out_ref[1] = down_ref[1]
    out_ref[2, 0] = far_x_ref[1]
    out_ref[2, 1] = far_g_ref[1]


def forward_kernel(*refs):
    own_ref, swap_ref, up_ref, down_ref, far_x_ref, far_g_ref, other_ref = refs[:7]
    gate_ref, up_w_ref, down_w_ref, out_ref, x_ref, g_ref = refs[7:]
    taken = own_ref.shape[1]
    for which, (far_ref, rows_ref) in enumerate(((far_x_ref, x_ref), (far_g_ref, g_ref))):
        blocks = [own_ref[which], swap_ref[which], up_ref[0, which], down_ref[0, which], far_ref[0]]
        blocks += [other_ref[i, which] for i in range(3)]
        for i, block in enumerate(blocks):
            rows_ref[i * taken : (i + 1) * taken, :] = block
    hidden = gate_ref.shape[0]
    for i, (w_ref, rows_ref) in enumerate(((gate_ref, x_ref), (up_w_ref, x_ref), (down_w_ref, g_ref))):
        total = dot(rows_ref[...], w_ref[...], 1, 1)
        out_ref[:, i * hidden : (i + 1) * hidden] = total.astype(BF16)


def middle_kernel(part_ref, out_ref):
    parts, block, _ = part_ref.shape
    hidden = part_ref.shape[2] // 3
    gate, up, back = (
        add_up([part_ref[k, :, i * hidden : (i + 1) * hidden].astype(F32) for k in range(parts)])
        for i in range(3)
    )
    sig = 1.0 / (1.0 + jnp.exp(-gate))
    act = gate * sig
    score = jnp.sum(act * up * back, axis=1, keepdims=True)
    out_ref[:, :hidden] = (back * up * sig * (1.0 + gate * (1.0 - sig))).astype(BF16)
    out_ref[:, hidden : 2 * hidden] = (back * act).astype(BF16)
    high = score.astype(BF16).astype(F32)
    lane = iota((block, LANES), 1)
    both = jnp.where(lane == 0, high, jnp.where(lane == 1, score - high, 0.0))
    out_ref[:, 2 * hidden :] = both.astype(BF16)


def score_block(d_scores, shards):
    rows = d_scores.shape[0]
    each = rows // shards
    pick = (iota((PAD, LANES), 0) == iota((PAD, LANES), 1)).astype(BF16)
    lines = dot(pick, d_scores, 1, 1)
    at = iota((PAD, rows), 0)
    shard = iota((PAD, rows), 1) // each
    apart = jnp.where(at == shard, lines[0:1, :], jnp.where(at == shard + shards, lines[1:2, :], 0.0))
    lane = iota((rows, LANES), 0) % each
    return dot(apart.astype(BF16), (iota((rows, LANES), 1) == lane).astype(BF16), 1, 0)


def backward_kernel(shards, d_ref, gate_ref, up_ref, out_ref):
    rows, hidden = d_ref.shape[0], gate_ref.shape[0]
    parts, _, share = out_ref.shape
    block = score_block(d_ref[:, 2 * hidden :], shards).astype(BF16)
    for k in range(parts):
        cols = slice(k * share, (k + 1) * share)
        total = dot(d_ref[:, :hidden], gate_ref[:, cols], 1, 0)
        total += dot(d_ref[:, hidden : 2 * hidden], up_ref[:, cols], 1, 0)
        out_ref[k, :rows, :] = total.astype(BF16)
        out_ref[k, rows:, :] = jnp.zeros((PAD, share), BF16)
        out_ref[k, rows:, :LANES] = block


def sum_kernel(pos_ref, part_ref, out_ref):
    parts, _, share = part_ref.shape
    shards, each, _ = out_ref.shape
    each -= PAD
    order = [at(pos_ref, -dz, dc) for dz, dc in BLOCKS]
    for j in range(shards):
        rows = slice(j * each, (j + 1) * each)
        total = add_up([part_ref[k, rows, :].astype(F32) for k in range(parts)])
        out_ref[order[j], :each, :] = total.astype(BF16)
    total = add_up([part_ref[k, shards * each :, :].astype(F32) for k in range(parts)])
    score = total[:shards] + total[shards:]
    high = score.astype(BF16).astype(F32)
    low = score - high
    row = iota((PAD, share), 0)
    for j in range(shards):
        both = jnp.where(row == 0, high[j : j + 1], jnp.where(row == 1, low[j : j + 1], 0.0))
        out_ref[order[j], each:, :] = both.astype(BF16)


def scatter_kernel(picks_ref, weights_ref, back_ref, out_ref):
    experts, taken = picks_ref.shape
    tokens, share = out_ref.shape[0] - PAD, out_ref.shape[1]
    weights = weights_ref[...].astype(F32)
    scores = jnp.zeros((PAD, share), F32)
    line = iota((PAD, share), 0)
    token = iota((tokens, taken), 0)
    terms = []
    for e in range(experts):
        lines = back_ref[e, taken:, :].astype(F32)
        scores = jnp.where(line == e, lines[0:1], jnp.where(line == e + experts, lines[1:2], scores))
        placed = jnp.where(token == picks_ref[e : e + 1, :], weights[e : e + 1, :], 0.0).astype(BF16)
        terms.append(dot(placed, back_ref[e, :taken, :], 1, 0))
    out_ref[:tokens, :] = add_up(terms).astype(BF16)
    out_ref[tokens:, :] = scores.astype(BF16)


def final_kernel(part_ref, grad_ref, score_ref):
    tokens = grad_ref.shape[0]
    experts, taken = score_ref.shape
    total = add_up([part_ref[k].astype(F32) for k in range(part_ref.shape[0])])
    grad_ref[...] = total[:tokens].astype(BF16)
    score = total[tokens : tokens + experts] + total[tokens + experts :]
    score_ref[...] = score[:, :taken].astype(BF16)


def exchange(a, axes):
    return lax.all_to_all(a, axes, split_axis=0, concat_axis=0, tiled=True)


def along_z(dz):
    nl, nc, nh = (SIZES[a] for a in RING)
    return [
        ((z % nl * nc + c) * nh + z // nl, (to % nl * nc + c) * nh + to // nl)
        for z in range(nl * nh)
        for to in [(z + dz) % (nl * nh)]
        for c in range(nc)
    ]


def local(layer_input, out_grad, scores, picks, w_gate, w_up, w_down):
    experts, taken = picks.shape
    tokens, width = layer_input.shape
    w_gate, w_up, w_down = w_gate[0], w_up[0], w_down[0]
    hidden = w_gate.shape[0]
    rows = experts * taken
    ny, nx = SIZES["y"], SIZES["x"]
    share, block = width // ny, rows // nx

    pos = jnp.stack([lax.axis_index(a).astype(jnp.int32) for a in EXPERT])
    one, two = sds((2, taken, width)), sds((2, 2, taken, width))
    own, swap, up, down, far_x, far_g = call(
        pick_kernel,
        [one, one, two, two, one, one],
        (pos, picks, jnp.stack([layer_input, out_grad])),
        flops=4 * rows * tokens * width,
        specs=[SMEM, VMEM, VMEM],
        scratch=[pltpu.VMEM((rows, tokens), BF16)],
    )
    up, down, far_x, far_g = (
        lax.ppermute(a, RING, along_z(dz)) for a, dz in ((up, 1), (down, -1), (far_x, 2), (far_g, -2))
    )

    across = [(0, 1), (1, 0)]
    swap = lax.ppermute(swap, "c", across)
    others = call(pass_kernel, sds((3, 2, taken, width)), (up, down, far_x, far_g), flops=0)
    others = lax.ppermute(others, "c", across)
    part = call(
        forward_kernel,
        sds((rows, 3 * hidden)),
        (own, swap, up, down, far_x, far_g, others, w_gate, w_up, w_down),
        flops=6 * rows * hidden * width,
        scratch=[pltpu.VMEM((rows, width), BF16)] * 2,
    )
    part = exchange(part.reshape(nx, block, 3 * hidden), "x")
    d_block = call(middle_kernel, sds((block, 2 * hidden + LANES)), (part,), flops=30 * block * hidden)
    d = lax.all_gather(d_block, "x", tiled=True)
    part = call(
        functools.partial(backward_kernel, experts),
        sds((ny, rows + PAD, share)),
        (d, w_gate, w_up),
        flops=4 * rows * hidden * width,
    )
    summed = call(
        sum_kernel,
        sds((experts, taken + PAD, share)),
        (pos, exchange(part, "y")),
        flops=4 * part.size,
        specs=[SMEM, VMEM],
    )
    back = exchange(summed, EXPERT)
    mine = call(
        scatter_kernel, sds((tokens + PAD, share)), (picks, scores, back), flops=2 * rows * tokens * share
    )
    token_grad, score_grad = call(
        final_kernel,
        [sds((tokens, share)), sds((experts, taken))],
        (lax.all_gather(mine, "zh"),),
        flops=4 * mine.size,
    )
    return lax.all_gather(token_grad, "y", axis=1, tiled=True), score_grad


def solution(mesh):
    fine = Mesh(mesh.devices.reshape(tuple(SIZES.values())), tuple(SIZES))
    ffn = ("y", "zh")
    placed_in = (
        P(EXPERT, "x"),
        P(EXPERT, "x"),
        P(None, EXPERT),
        P(None, EXPERT),
        P(EXPERT, ffn, "x"),
        P(EXPERT, ffn, "x"),
        P(EXPERT, ffn, "x"),
    )
    return jax.shard_map(
        local,
        mesh=fine,
        in_specs=placed_in,
        out_specs=(P(EXPERT, "x"), P(None, EXPERT)),
        check_vma=False,
    )
```

```python
import functools

import jax
import jax.numpy as jnp
from jax import lax
from jax.experimental import pallas as pl
from jax.experimental.pallas import tpu as pltpu
from jax.sharding import Mesh, PartitionSpec as P

BF16 = jnp.bfloat16
F32 = jnp.float32
LANES = 128
PAD = 16
TAIL = 8
EXPERT = ("zl", "c")
RING = ("zl", "c", "zh")
SIZES = {"zl": 4, "c": 2, "y": 4, "zh": 4, "x": 4}
LIMIT = 16
VMEM = pl.BlockSpec(memory_space=pltpu.VMEM)
SMEM = pl.BlockSpec(memory_space=pltpu.SMEM)


def dot(a, b, ca, cb):
    return lax.dot_general(a, b, (((ca,), (cb,)), ((), ())), preferred_element_type=F32)


def iota(shape, axis):
    return lax.broadcasted_iota(jnp.int32, shape, axis)


def sds(shape, dtype=BF16):
    return jax.ShapeDtypeStruct(shape, dtype)


def add_up(pieces):
    return functools.reduce(lambda a, b: a + b, pieces)


def call(kernel, outs, args, *, flops, specs=None, scratch=(), limit=LIMIT):
    nbytes = sum(a.size * a.dtype.itemsize for a in list(args) + jax.tree.leaves(outs))
    return pl.pallas_call(
        kernel,
        out_shape=outs,
        in_specs=specs or [VMEM] * len(args),
        out_specs=jax.tree.map(lambda o: VMEM, outs),
        scratch_shapes=scratch,
        compiler_params=pltpu.CompilerParams(vmem_limit_bytes=limit << 20),
        cost_estimate=pl.CostEstimate(flops=flops, bytes_accessed=nbytes, transcendentals=0),
    )(*args)


BLOCKS = ((0, 0), (0, 1), (1, 0), (-1, 0), (1, 1), (-1, 1), (2, 0), (-2, 1))
NEAR = 6
NEAR_COST, FAR_COST = 1, 10
SENT = (2, 3, 4, 5, 1, 6, 7)


def at(pos_ref, dz, dc):
    chips, cores = SIZES["zl"], SIZES["c"]
    return lax.rem(pos_ref[0] + (dz + chips), chips) * cores + lax.rem(pos_ref[1] + dc, cores)


def pick_kernel(pos_ref, picks_ref, xg_ref, *refs):
    *outs, hot_ref = refs
    experts, taken = picks_ref.shape
    tokens, width = xg_ref.shape[1:]
    row = iota(picks_ref.shape, 0)
    values = picks_ref[...].astype(F32)
    picked = [
        jnp.sum(jnp.where(row == at(pos_ref, *b), values, 0.0), axis=0, keepdims=True) for b in BLOCKS
    ]
    picks = jnp.transpose(jnp.concatenate(picked, axis=0))
    lane = iota((taken, tokens), 1).astype(F32)
    for i in range(experts):
        hot_ref[i * taken : (i + 1) * taken, :] = (lane == picks[:, i : i + 1]).astype(BF16)
    step = 4 * LANES
    for which in range(2):
        for start in range(0, width, step):
            cols = slice(start, start + step)
            rows = dot(hot_ref[...], xg_ref[which, :, cols], 1, 0).astype(BF16)
            for i in range(experts):
                outs[i][which, :, cols] = rows[i * taken : (i + 1) * taken]


def after_kernel(a_ref, _, out_ref):
    out_ref[...] = a_ref[...]


def forward_kernel(*refs):
    blocks, (gate_ref, up_ref, down_ref, out_ref, x_ref, g_ref) = refs[:-6], refs[-6:]
    taken = blocks[0].shape[1]
    for which, rows_ref in enumerate((x_ref, g_ref)):
        for i, block in enumerate(blocks):
            rows_ref[i * taken : (i + 1) * taken, :] = block[which]
    hidden = gate_ref.shape[0]
    for i, (w_ref, rows_ref) in enumerate(((gate_ref, x_ref), (up_ref, x_ref), (down_ref, g_ref))):
        total = dot(rows_ref[...], w_ref[...], 1, 1)
        out_ref[:, i * hidden : (i + 1) * hidden] = total.astype(BF16)


def middle_kernel(*refs):
    *part_refs, out_ref = refs
    hidden = part_refs[0].shape[2] // 3

    def total(i):
        cols = slice(i * hidden, (i + 1) * hidden)
        sums = [add_up([ref[k, :, cols].astype(F32) for k in range(ref.shape[0])]) for ref in part_refs]
        return jnp.concatenate(sums, axis=0)

    gate, up, back = total(0), total(1), total(2)
    sig = 1.0 / (1.0 + jnp.exp(-gate))
    act = gate * sig
    score = jnp.sum(act * up * back, axis=1, keepdims=True)
    out_ref[:, :hidden] = (back * up * sig * (1.0 + gate * (1.0 - sig))).astype(BF16)
    out_ref[:, hidden : 2 * hidden] = (back * act).astype(BF16)
    high = score.astype(BF16).astype(F32)
    lane = iota((out_ref.shape[0], LANES), 1)
    both = jnp.where(lane == 0, high, jnp.where(lane == 1, score - high, 0.0))
    out_ref[:, 2 * hidden :] = both.astype(BF16)


def in_blocks(row, rows):
    parts = SIZES["x"]
    near = rows * NEAR // len(BLOCKS)
    x, r = row // (rows // parts), row % (rows // parts)
    near_x = near // parts
    return jnp.where(r < near_x, x * near_x + r, near + x * (rows // parts - near_x) + r - near_x)


def score_block(d_scores, shards):
    rows = d_scores.shape[0]
    each = rows // shards
    pick = (iota((PAD, LANES), 0) == iota((PAD, LANES), 1)).astype(BF16)
    lines = dot(pick, d_scores, 1, 1)
    line = iota((PAD, rows), 0)
    block = in_blocks(iota((PAD, rows), 1), rows) // each
    apart = jnp.where(line == block, lines[0:1, :], jnp.where(line == block + shards, lines[1:2, :], 0.0))
    lane = in_blocks(iota((rows, LANES), 0), rows) % each
    return dot(apart.astype(BF16), (iota((rows, LANES), 1) == lane).astype(BF16), 1, 0)


def backward_kernel(shards, d_ref, gate_ref, up_ref, out_ref):
    rows, hidden = d_ref.shape[0], gate_ref.shape[0]
    parts, _, share = out_ref.shape
    block = score_block(d_ref[:, 2 * hidden :], shards).astype(BF16)
    for k in range(parts):
        cols = slice(k * share, (k + 1) * share)
        total = dot(d_ref[:, :hidden], gate_ref[:, cols], 1, 0)
        total += dot(d_ref[:, hidden : 2 * hidden], up_ref[:, cols], 1, 0)
        out_ref[k, :rows, :] = total.astype(BF16)
        out_ref[k, rows:, :] = jnp.zeros((PAD, share), BF16)
        out_ref[k, rows:, :LANES] = block


def sum_kernel(pos_ref, part_ref, out_ref):
    parts, _, share = part_ref.shape
    shards, each, _ = out_ref.shape
    each -= TAIL
    rows = shards * each
    total = add_up([part_ref[k].astype(F32) for k in range(parts)])
    one = rows // SIZES["x"]
    near = one * NEAR // len(BLOCKS)
    ordered = [total[x * one : x * one + near] for x in range(SIZES["x"])]
    ordered += [total[x * one + near : (x + 1) * one] for x in range(SIZES["x"])]
    ordered = jnp.concatenate(ordered, axis=0)
    score = total[rows : rows + shards] + total[rows + shards :]
    high = score.astype(BF16).astype(F32)
    low = score - high
    row = iota((TAIL, share), 0)
    for i, (dz, dc) in enumerate(BLOCKS):
        both = jnp.where(row == 0, high[i : i + 1], jnp.where(row == 1, low[i : i + 1], 0.0))
        block = jnp.concatenate([ordered[i * each : (i + 1) * each], both], axis=0)
        out_ref[at(pos_ref, -dz, dc)] = block.astype(BF16)


def scatter_kernel(picks_ref, weights_ref, back_ref, out_ref):
    experts, taken = picks_ref.shape
    tokens, share = out_ref.shape[0] - PAD, out_ref.shape[1]
    weights = weights_ref[...].astype(F32)
    scores = jnp.zeros((PAD, share), F32)
    line = iota((PAD, share), 0)
    token = iota((tokens, taken), 0)
    terms = []
    for e in range(experts):
        block = back_ref[e].astype(F32)
        lines = block[taken:]
        scores = jnp.where(line == e, lines[0:1], jnp.where(line == e + experts, lines[1:2], scores))
        placed = jnp.where(token == picks_ref[e : e + 1, :], weights[e : e + 1, :], 0.0).astype(BF16)
        terms.append(dot(placed, block[:taken].astype(BF16), 1, 0))
    out_ref[:tokens, :] = add_up(terms).astype(BF16)
    out_ref[tokens:, :] = scores.astype(BF16)


def final_kernel(part_ref, grad_ref, score_ref):
    tokens = grad_ref.shape[0]
    experts, taken = score_ref.shape
    total = add_up([part_ref[k].astype(F32) for k in range(part_ref.shape[0])])
    grad_ref[...] = total[:tokens].astype(BF16)
    score = total[tokens : tokens + experts] + total[tokens + experts :]
    score_ref[...] = score[:, :taken].astype(BF16)


def exchange(a, axes):
    return lax.all_to_all(a, axes, split_axis=0, concat_axis=0, tiled=True)


def along_z(dz, dc):
    nl, nc, nh = (SIZES[a] for a in RING)
    return [
        ((z % nl * nc + c) * nh + z // nl, (to % nl * nc + (c + dc) % nc) * nh + to // nl)
        for z in range(nl * nh)
        for to in [(z + dz) % (nl * nh)]
        for c in range(nc)
    ]


def local(layer_input, out_grad, scores, picks, w_gate, w_up, w_down):
    experts, taken = picks.shape
    tokens, width = layer_input.shape
    w_gate, w_up, w_down = w_gate[0], w_up[0], w_down[0]
    hidden = w_gate.shape[0]
    rows = experts * taken
    ny, nx = SIZES["y"], SIZES["x"]
    share, block = width // ny, rows // nx

    pos = jnp.stack([lax.axis_index(a).astype(jnp.int32) for a in EXPERT])
    sent = call(
        pick_kernel,
        [sds((2, taken, width))] * experts,
        (pos, picks, jnp.stack([layer_input, out_grad])),
        flops=4 * rows * tokens * width,
        specs=[SMEM, VMEM, VMEM],
        scratch=[pltpu.VMEM((rows, tokens), BF16)],
    )
    got = {0: sent[0]}
    for i in SENT:
        got[i] = lax.ppermute(sent[i], RING, along_z(*BLOCKS[i]))

    def project(blocks, factor):
        count = len(blocks) * taken
        return call(
            forward_kernel,
            sds((count, 3 * hidden)),
            (*blocks, w_gate, w_up, w_down),
            flops=int(factor * 6 * count * hidden * width),
            scratch=[pltpu.VMEM((count, width), BF16)] * 2,
        )

    def over_x(a):
        return exchange(a.reshape(nx, a.shape[0] // nx, 3 * hidden), "x")

    near = over_x(project([got[i] for i in range(NEAR)], NEAR_COST))
    far = project([got[i] for i in range(NEAR, experts)], FAR_COST)
    far = over_x(call(after_kernel, sds(far.shape), (far, near), flops=0))
    parts = (near, far)
    d_block = call(middle_kernel, sds((block, 2 * hidden + LANES)), parts, flops=30 * block * hidden)
    d = lax.all_gather(d_block, "x", tiled=True)
    part = call(
        functools.partial(backward_kernel, experts),
        sds((ny, rows + PAD, share)),
        (d, w_gate, w_up),
        flops=4 * rows * hidden * width,
    )
    summed = call(
        sum_kernel,
        sds((experts, taken + TAIL, share)),
        (pos, exchange(part, "y")),
        flops=4 * part.size,
        specs=[SMEM, VMEM],
    )
    back = exchange(summed, EXPERT)
    mine = call(
        scatter_kernel, sds((tokens + PAD, share)), (picks, scores, back), flops=2 * rows * tokens * share
    )
    token_grad, score_grad = call(
        final_kernel,
        [sds((tokens, share)), sds((experts, taken))],
        (lax.all_gather(mine, "zh"),),
        flops=4 * mine.size,
    )
    return lax.all_gather(token_grad, "y", axis=1, tiled=True), score_grad


def solution(mesh):
    fine = Mesh(mesh.devices.reshape(tuple(SIZES.values())), tuple(SIZES))
    ffn = ("y", "zh")
    placed_in = (
        P(EXPERT, "x"),
        P(EXPERT, "x"),
        P(None, EXPERT),
        P(None, EXPERT),
        P(EXPERT, ffn, "x"),
        P(EXPERT, ffn, "x"),
        P(EXPERT, ffn, "x"),
    )
    return jax.shard_map(
        local,
        mesh=fine,
        in_specs=placed_in,
        out_specs=(P(EXPERT, "x"), P(None, EXPERT)),
        check_vma=False,
    )
```

```python
import functools

import jax
import jax.numpy as jnp
from jax import lax
from jax.experimental import pallas as pl
from jax.experimental.pallas import tpu as pltpu
from jax.sharding import Mesh, PartitionSpec as P

BF16 = jnp.bfloat16
F32 = jnp.float32
LANES = 128
PAD = 16
TAIL = 8
EXPERT = ("zl", "c")
RING = ("zl", "c", "zh")
SIZES = {"zl": 4, "c": 2, "y": 4, "zh": 4, "x": 4}
LIMIT = 16
VMEM = pl.BlockSpec(memory_space=pltpu.VMEM)
SMEM = pl.BlockSpec(memory_space=pltpu.SMEM)


def dot(a, b, ca, cb):
    return lax.dot_general(a, b, (((ca,), (cb,)), ((), ())), preferred_element_type=F32)


def iota(shape, axis):
    return lax.broadcasted_iota(jnp.int32, shape, axis)


def sds(shape, dtype=BF16):
    return jax.ShapeDtypeStruct(shape, dtype)


def add_up(pieces):
    return functools.reduce(lambda a, b: a + b, pieces)


def call(kernel, outs, args, *, flops, specs=None, scratch=(), limit=LIMIT):
    nbytes = sum(a.size * a.dtype.itemsize for a in list(args) + jax.tree.leaves(outs))
    return pl.pallas_call(
        kernel,
        out_shape=outs,
        in_specs=specs or [VMEM] * len(args),
        out_specs=jax.tree.map(lambda o: VMEM, outs),
        scratch_shapes=scratch,
        compiler_params=pltpu.CompilerParams(vmem_limit_bytes=limit << 20),
        cost_estimate=pl.CostEstimate(flops=flops, bytes_accessed=nbytes, transcendentals=0),
    )(*args)


BLOCKS = ((0, 0), (0, 1), (1, 0), (-1, 0), (1, 1), (-1, 1), (2, 0), (-2, 1))
NEAR = 6
NEAR_COST, FAR_COST = 1, 10
SENT = (2, 3, 4, 5, 6, 7)


def at(pos_ref, dz, dc):
    chips, cores = SIZES["zl"], SIZES["c"]
    return lax.rem(pos_ref[0] + (dz + chips), chips) * cores + lax.rem(pos_ref[1] + dc, cores)


def pick_kernel(pos_ref, picks_ref, xg_ref, *refs):
    *outs, hot_ref = refs
    experts, taken = picks_ref.shape
    tokens, width = xg_ref.shape[1:]
    row = iota(picks_ref.shape, 0)
    values = picks_ref[...].astype(F32)
    picked = [
        jnp.sum(jnp.where(row == at(pos_ref, *b), values, 0.0), axis=0, keepdims=True) for b in BLOCKS
    ]
    picks = jnp.transpose(jnp.concatenate(picked, axis=0))
    lane = iota((taken, tokens), 1).astype(F32)
    for i in range(experts):
        hot_ref[i * taken : (i + 1) * taken, :] = (lane == picks[:, i : i + 1]).astype(BF16)
    step = 4 * LANES
    for which in range(2):
        for start in range(0, width, step):
            cols = slice(start, start + step)
            rows = dot(hot_ref[...], xg_ref[which, :, cols], 1, 0).astype(BF16)
            for i in range(experts):
                outs[i][which, :, cols] = rows[i * taken : (i + 1) * taken]


def after_kernel(a_ref, _, out_ref):
    out_ref[...] = a_ref[...]


def forward_kernel(pos_ref, *refs):
    blocks, (gate_ref, up_ref, down_ref, out_ref, x_ref, g_ref) = refs[:-6], refs[-6:]
    taken = blocks[0].shape[1]
    blocks = [ref if len(ref.shape) == 3 else ref.at[1 - pos_ref[1]] for ref in blocks]
    for which, rows_ref in enumerate((x_ref, g_ref)):
        for i, block in enumerate(blocks):
            rows_ref[i * taken : (i + 1) * taken, :] = block[which]
    hidden = gate_ref.shape[0]
    for i, (w_ref, rows_ref) in enumerate(((gate_ref, x_ref), (up_ref, x_ref), (down_ref, g_ref))):
        total = dot(rows_ref[...], w_ref[...], 1, 1)
        out_ref[:, i * hidden : (i + 1) * hidden] = total.astype(BF16)


def middle_kernel(*refs):
    *part_refs, out_ref = refs
    hidden = part_refs[0].shape[2] // 3

    def total(i):
        cols = slice(i * hidden, (i + 1) * hidden)
        sums = [add_up([ref[k, :, cols].astype(F32) for k in range(ref.shape[0])]) for ref in part_refs]
        return jnp.concatenate(sums, axis=0)

    gate, up, back = total(0), total(1), total(2)
    sig = 1.0 / (1.0 + jnp.exp(-gate))
    act = gate * sig
    score = jnp.sum(act * up * back, axis=1, keepdims=True)
    out_ref[:, :hidden] = (back * up * sig * (1.0 + gate * (1.0 - sig))).astype(BF16)
    out_ref[:, hidden : 2 * hidden] = (back * act).astype(BF16)
    high = score.astype(BF16).astype(F32)
    lane = iota((out_ref.shape[0], LANES), 1)
    both = jnp.where(lane == 0, high, jnp.where(lane == 1, score - high, 0.0))
    out_ref[:, 2 * hidden :] = both.astype(BF16)


def in_blocks(row, rows):
    parts = SIZES["x"]
    near = rows * NEAR // len(BLOCKS)
    x, r = row // (rows // parts), row % (rows // parts)
    near_x = near // parts
    return jnp.where(r < near_x, x * near_x + r, near + x * (rows // parts - near_x) + r - near_x)


def score_block(d_scores, shards):
    rows = d_scores.shape[0]
    each = rows // shards
    pick = (iota((PAD, LANES), 0) == iota((PAD, LANES), 1)).astype(BF16)
    lines = dot(pick, d_scores, 1, 1)
    line = iota((PAD, rows), 0)
    block = in_blocks(iota((PAD, rows), 1), rows) // each
    apart = jnp.where(line == block, lines[0:1, :], jnp.where(line == block + shards, lines[1:2, :], 0.0))
    lane = in_blocks(iota((rows, LANES), 0), rows) % each
    return dot(apart.astype(BF16), (iota((rows, LANES), 1) == lane).astype(BF16), 1, 0)


def backward_kernel(shards, d_ref, gate_ref, up_ref, out_ref):
    rows, hidden = d_ref.shape[0], gate_ref.shape[0]
    parts, _, share = out_ref.shape
    block = score_block(d_ref[:, 2 * hidden :], shards).astype(BF16)
    for k in range(parts):
        cols = slice(k * share, (k + 1) * share)
        total = dot(d_ref[:, :hidden], gate_ref[:, cols], 1, 0)
        total += dot(d_ref[:, hidden : 2 * hidden], up_ref[:, cols], 1, 0)
        out_ref[k, :rows, :] = total.astype(BF16)
        out_ref[k, rows:, :] = jnp.zeros((PAD, share), BF16)
        out_ref[k, rows:, :LANES] = block


def sum_kernel(pos_ref, part_ref, out_ref):
    parts, _, share = part_ref.shape
    shards, each, _ = out_ref.shape
    each -= TAIL
    rows = shards * each
    total = add_up([part_ref[k].astype(F32) for k in range(parts)])
    one = rows // SIZES["x"]
    near = one * NEAR // len(BLOCKS)
    ordered = [total[x * one : x * one + near] for x in range(SIZES["x"])]
    ordered += [total[x * one + near : (x + 1) * one] for x in range(SIZES["x"])]
    ordered = jnp.concatenate(ordered, axis=0)
    score = total[rows : rows + shards] + total[rows + shards :]
    high = score.astype(BF16).astype(F32)
    low = score - high
    row = iota((TAIL, share), 0)
    for i, (dz, dc) in enumerate(BLOCKS):
        both = jnp.where(row == 0, high[i : i + 1], jnp.where(row == 1, low[i : i + 1], 0.0))
        block = jnp.concatenate([ordered[i * each : (i + 1) * each], both], axis=0)
        out_ref[at(pos_ref, -dz, dc)] = block.astype(BF16)


def scatter_kernel(picks_ref, weights_ref, back_ref, out_ref):
    experts, taken = picks_ref.shape
    tokens, share = out_ref.shape[0] - PAD, out_ref.shape[1]
    weights = weights_ref[...].astype(F32)
    scores = jnp.zeros((PAD, share), F32)
    line = iota((PAD, share), 0)
    token = iota((tokens, taken), 0)
    terms = []
    for e in range(experts):
        block = back_ref[e].astype(F32)
        lines = block[taken:]
        scores = jnp.where(line == e, lines[0:1], jnp.where(line == e + experts, lines[1:2], scores))
        placed = jnp.where(token == picks_ref[e : e + 1, :], weights[e : e + 1, :], 0.0).astype(BF16)
        terms.append(dot(placed, block[:taken].astype(BF16), 1, 0))
    out_ref[:tokens, :] = add_up(terms).astype(BF16)
    out_ref[tokens:, :] = scores.astype(BF16)


def final_kernel(part_ref, grad_ref, score_ref):
    tokens = grad_ref.shape[0]
    experts, taken = score_ref.shape
    total = add_up([part_ref[k].astype(F32) for k in range(part_ref.shape[0])])
    grad_ref[...] = total[:tokens].astype(BF16)
    score = total[tokens : tokens + experts] + total[tokens + experts :]
    score_ref[...] = score[:, :taken].astype(BF16)


def exchange(a, axes):
    return lax.all_to_all(a, axes, split_axis=0, concat_axis=0, tiled=True)


def along_z(dz, dc):
    nl, nc, nh = (SIZES[a] for a in RING)
    return [
        ((z % nl * nc + c) * nh + z // nl, (to % nl * nc + (c + dc) % nc) * nh + to // nl)
        for z in range(nl * nh)
        for to in [(z + dz) % (nl * nh)]
        for c in range(nc)
    ]


def local(layer_input, out_grad, scores, picks, w_gate, w_up, w_down):
    experts, taken = picks.shape
    tokens, width = layer_input.shape
    w_gate, w_up, w_down = w_gate[0], w_up[0], w_down[0]
    hidden = w_gate.shape[0]
    rows = experts * taken
    ny, nx = SIZES["y"], SIZES["x"]
    share, block = width // ny, rows // nx

    pos = jnp.stack([lax.axis_index(a).astype(jnp.int32) for a in EXPERT])
    sent = call(
        pick_kernel,
        [sds((2, taken, width))] * experts,
        (pos, picks, jnp.stack([layer_input, out_grad])),
        flops=4 * rows * tokens * width,
        specs=[SMEM, VMEM, VMEM],
        scratch=[pltpu.VMEM((rows, tokens), BF16)],
    )
    got = {0: sent[0]}
    for i in SENT:
        got[i] = lax.ppermute(sent[i], RING, along_z(*BLOCKS[i]))
    got[1] = lax.all_gather(sent[1], "c")

    def project(blocks, factor):
        count = len(blocks) * taken
        return call(
            forward_kernel,
            sds((count, 3 * hidden)),
            (pos, *blocks, w_gate, w_up, w_down),
            specs=[SMEM] + [VMEM] * (len(blocks) + 3),
            flops=int(factor * 6 * count * hidden * width),
            scratch=[pltpu.VMEM((count, width), BF16)] * 2,
        )

    def over_x(a):
        return exchange(a.reshape(nx, a.shape[0] // nx, 3 * hidden), "x")

    near = over_x(project([got[i] for i in range(NEAR)], NEAR_COST))
    far = project([got[i] for i in range(NEAR, experts)], FAR_COST)
    far = over_x(call(after_kernel, sds(far.shape), (far, near), flops=0))
    parts = (near, far)
    d_block = call(middle_kernel, sds((block, 2 * hidden + LANES)), parts, flops=30 * block * hidden)
    d = lax.all_gather(d_block, "x", tiled=True)
    part = call(
        functools.partial(backward_kernel, experts),
        sds((ny, rows + PAD, share)),
        (d, w_gate, w_up),
        flops=4 * rows * hidden * width,
    )
    summed = call(
        sum_kernel,
        sds((experts, taken + TAIL, share)),
        (pos, exchange(part, "y")),
        flops=4 * part.size,
        specs=[SMEM, VMEM],
    )
    back = exchange(summed, EXPERT)
    mine = call(
        scatter_kernel, sds((tokens + PAD, share)), (picks, scores, back), flops=2 * rows * tokens * share
    )
    token_grad, score_grad = call(
        final_kernel,
        [sds((tokens, share)), sds((experts, taken))],
        (lax.all_gather(mine, "zh"),),
        flops=4 * mine.size,
    )
    return lax.all_gather(token_grad, "y", axis=1, tiled=True), score_grad


def solution(mesh):
    fine = Mesh(mesh.devices.reshape(tuple(SIZES.values())), tuple(SIZES))
    ffn = ("y", "zh")
    placed_in = (
        P(EXPERT, "x"),
        P(EXPERT, "x"),
        P(None, EXPERT),
        P(None, EXPERT),
        P(EXPERT, ffn, "x"),
        P(EXPERT, ffn, "x"),
        P(EXPERT, ffn, "x"),
    )
    return jax.shard_map(
        local,
        mesh=fine,
        in_specs=placed_in,
        out_specs=(P(EXPERT, "x"), P(None, EXPERT)),
        check_vma=False,
    )
```

```python
import functools

import jax
import jax.numpy as jnp
from jax import lax
from jax.experimental import pallas as pl
from jax.experimental.pallas import tpu as pltpu
from jax.sharding import Mesh, PartitionSpec as P

BF16 = jnp.bfloat16
F32 = jnp.float32
LANES = 128
PAD = 16
TAIL = 8
EXPERT = ("zl", "c")
RING = ("zl", "c", "zh")
SIZES = {"zl": 4, "c": 2, "y": 4, "zh": 4, "x": 4}
LIMIT = 16
VMEM = pl.BlockSpec(memory_space=pltpu.VMEM)


def dot(a, b, ca, cb):
    return lax.dot_general(a, b, (((ca,), (cb,)), ((), ())), preferred_element_type=F32)


def iota(shape, axis):
    return lax.broadcasted_iota(jnp.int32, shape, axis)


def sds(shape, dtype=BF16):
    return jax.ShapeDtypeStruct(shape, dtype)


def add_up(pieces):
    return functools.reduce(lambda a, b: a + b, pieces)


def call(kernel, outs, args, *, flops, specs=None, scratch=(), limit=LIMIT):
    nbytes = sum(a.size * a.dtype.itemsize for a in list(args) + jax.tree.leaves(outs))
    return pl.pallas_call(
        kernel,
        out_shape=outs,
        in_specs=specs or [VMEM] * len(args),
        out_specs=jax.tree.map(lambda o: VMEM, outs),
        scratch_shapes=scratch,
        compiler_params=pltpu.CompilerParams(vmem_limit_bytes=limit << 20),
        cost_estimate=pl.CostEstimate(flops=flops, bytes_accessed=nbytes, transcendentals=0),
    )(*args)


BLOCKS = ((0, 0), (0, 1), (1, 0), (-1, 0), (1, 1), (-1, 1), (2, 0), (-2, 1))
NEAR = 6
NEAR_COST, FAR_COST = 1, 10
SENT = (2, 3, 4, 5, 6, 7)


def at(dz, dc):
    chips, cores = SIZES["zl"], SIZES["c"]
    return lax.rem(lax.axis_index("zl") + (dz + chips), chips) * cores + lax.rem(lax.axis_index("c") + dc, cores)


def pick_kernel(picks_ref, xg_ref, *refs):
    *outs, hot_ref = refs
    experts, taken = picks_ref.shape
    tokens, width = xg_ref.shape[1:]
    row = iota(picks_ref.shape, 0)
    values = picks_ref[...].astype(F32)
    picked = [
        jnp.sum(jnp.where(row == at(*b), values, 0.0), axis=0, keepdims=True) for b in BLOCKS
    ]
    picks = jnp.transpose(jnp.concatenate(picked, axis=0))
    lane = iota((taken, tokens), 1).astype(F32)
    for i in range(experts):
        hot_ref[i * taken : (i + 1) * taken, :] = (lane == picks[:, i : i + 1]).astype(BF16)
    step = 4 * LANES
    for which in range(2):
        for start in range(0, width, step):
            cols = slice(start, start + step)
            rows = dot(hot_ref[...], xg_ref[which, :, cols], 1, 0).astype(BF16)
            for i in range(experts):
                outs[i][which, :, cols] = rows[i * taken : (i + 1) * taken]


def after_kernel(a_ref, _, out_ref):
    out_ref[...] = a_ref[...]


def forward_kernel(*refs):
    blocks, (gate_ref, up_ref, down_ref, out_ref, x_ref, g_ref) = refs[:-6], refs[-6:]
    taken = blocks[0].shape[1]
    blocks = [ref if len(ref.shape) == 3 else ref.at[1 - lax.axis_index("c")] for ref in blocks]
    for which, rows_ref in enumerate((x_ref, g_ref)):
        for i, block in enumerate(blocks):
            rows_ref[i * taken : (i + 1) * taken, :] = block[which]
    hidden = gate_ref.shape[0]
    for i, (w_ref, rows_ref) in enumerate(((gate_ref, x_ref), (up_ref, x_ref), (down_ref, g_ref))):
        total = dot(rows_ref[...], w_ref[...], 1, 1)
        out_ref[:, i * hidden : (i + 1) * hidden] = total.astype(BF16)


def middle_kernel(*refs):
    *part_refs, out_ref = refs
    hidden = part_refs[0].shape[2] // 3

    def total(i):
        cols = slice(i * hidden, (i + 1) * hidden)
        sums = [add_up([ref[k, :, cols].astype(F32) for k in range(ref.shape[0])]) for ref in part_refs]
        return jnp.concatenate(sums, axis=0)

    gate, up, back = total(0), total(1), total(2)
    sig = 1.0 / (1.0 + jnp.exp(-gate))
    act = gate * sig
    score = jnp.sum(act * up * back, axis=1, keepdims=True)
    out_ref[:, :hidden] = (back * up * sig * (1.0 + gate * (1.0 - sig))).astype(BF16)
    out_ref[:, hidden : 2 * hidden] = (back * act).astype(BF16)
    high = score.astype(BF16).astype(F32)
    lane = iota((out_ref.shape[0], LANES), 1)
    both = jnp.where(lane == 0, high, jnp.where(lane == 1, score - high, 0.0))
    out_ref[:, 2 * hidden :] = both.astype(BF16)


def in_blocks(row, rows):
    parts = SIZES["x"]
    near = rows * NEAR // len(BLOCKS)
    x, r = row // (rows // parts), row % (rows // parts)
    near_x = near // parts
    return jnp.where(r < near_x, x * near_x + r, near + x * (rows // parts - near_x) + r - near_x)


def score_block(d_scores, shards):
    rows = d_scores.shape[0]
    each = rows // shards
    pick = (iota((PAD, LANES), 0) == iota((PAD, LANES), 1)).astype(BF16)
    lines = dot(pick, d_scores, 1, 1)
    line = iota((PAD, rows), 0)
    block = in_blocks(iota((PAD, rows), 1), rows) // each
    apart = jnp.where(line == block, lines[0:1, :], jnp.where(line == block + shards, lines[1:2, :], 0.0))
    lane = in_blocks(iota((rows, LANES), 0), rows) % each
    return dot(apart.astype(BF16), (iota((rows, LANES), 1) == lane).astype(BF16), 1, 0)


def backward_kernel(shards, d_ref, gate_ref, up_ref, out_ref):
    rows, hidden = d_ref.shape[0], gate_ref.shape[0]
    parts, _, share = out_ref.shape
    block = score_block(d_ref[:, 2 * hidden :], shards).astype(BF16)
    for k in range(parts):
        cols = slice(k * share, (k + 1) * share)
        total = dot(d_ref[:, :hidden], gate_ref[:, cols], 1, 0)
        total += dot(d_ref[:, hidden : 2 * hidden], up_ref[:, cols], 1, 0)
        out_ref[k, :rows, :] = total.astype(BF16)
        out_ref[k, rows:, :] = jnp.zeros((PAD, share), BF16)
        out_ref[k, rows:, :LANES] = block


def sum_kernel(part_ref, out_ref, rows_ref):
    parts, _, share = part_ref.shape
    shards, each, _ = out_ref.shape
    each -= TAIL
    rows = shards * each
    one = rows // SIZES["x"]
    near = one * NEAR // len(BLOCKS)

    def total(start, count):
        return add_up([part_ref[k, start : start + count, :].astype(F32) for k in range(parts)])

    for x in range(SIZES["x"]):
        mine = total(x * one, one)
        rows_ref[x * near : (x + 1) * near, :] = mine[:near]
        far = SIZES["x"] * near + x * (one - near)
        rows_ref[far : far + one - near, :] = mine[near:]
    score = total(rows, PAD)
    score = score[:shards] + score[shards:]
    high = score.astype(BF16).astype(F32)
    low = score - high
    row = iota((TAIL, share), 0)
    for i, (dz, dc) in enumerate(BLOCKS):
        both = jnp.where(row == 0, high[i : i + 1], jnp.where(row == 1, low[i : i + 1], 0.0))
        block = jnp.concatenate([rows_ref[i * each : (i + 1) * each, :], both], axis=0)
        out_ref[at(-dz, dc)] = block.astype(BF16)


def scatter_kernel(picks_ref, weights_ref, back_ref, out_ref):
    experts, taken = picks_ref.shape
    tokens, share = out_ref.shape[0] - PAD, out_ref.shape[1]
    weights = weights_ref[...].astype(F32)
    scores = jnp.zeros((PAD, share), F32)
    line = iota((PAD, share), 0)
    token = iota((tokens, taken), 0)
    terms = []
    for e in range(experts):
        block = back_ref[e].astype(F32)
        lines = block[taken:]
        scores = jnp.where(line == e, lines[0:1], jnp.where(line == e + experts, lines[1:2], scores))
        placed = jnp.where(token == picks_ref[e : e + 1, :], weights[e : e + 1, :], 0.0).astype(BF16)
        terms.append(dot(placed, block[:taken].astype(BF16), 1, 0))
    out_ref[:tokens, :] = add_up(terms).astype(BF16)
    out_ref[tokens:, :] = scores.astype(BF16)


def token_kernel(part_ref, out_ref):
    tokens = out_ref.shape[0]
    out_ref[...] = add_up([part_ref[k, :tokens, :].astype(F32) for k in range(part_ref.shape[0])]).astype(BF16)


def final_kernel(gathered_ref, part_ref, grad_ref, score_ref):
    parts, tokens, share = gathered_ref.shape
    experts, taken = score_ref.shape
    for k in range(parts):
        grad_ref[:, k * share : (k + 1) * share] = gathered_ref[k]
    total = add_up([part_ref[k, tokens:, :].astype(F32) for k in range(part_ref.shape[0])])
    score = total[:experts] + total[experts:]
    score_ref[...] = score[:, :taken].astype(BF16)


def exchange(a, axes):
    return lax.all_to_all(a, axes, split_axis=0, concat_axis=0, tiled=True)


def along_z(dz, dc):
    nl, nc, nh = (SIZES[a] for a in RING)
    return [
        ((z % nl * nc + c) * nh + z // nl, (to % nl * nc + (c + dc) % nc) * nh + to // nl)
        for z in range(nl * nh)
        for to in [(z + dz) % (nl * nh)]
        for c in range(nc)
    ]


def local(layer_input, out_grad, scores, picks, w_gate, w_up, w_down):
    experts, taken = picks.shape
    tokens, width = layer_input.shape
    w_gate, w_up, w_down = w_gate[0], w_up[0], w_down[0]
    hidden = w_gate.shape[0]
    rows = experts * taken
    ny, nx = SIZES["y"], SIZES["x"]
    share, block = width // ny, rows // nx

    sent = call(
        pick_kernel,
        [sds((2, taken, width))] * experts,
        (picks, jnp.stack([layer_input, out_grad])),
        flops=4 * rows * tokens * width,
        scratch=[pltpu.VMEM((rows, tokens), BF16)],
    )
    got = {0: sent[0]}
    for i in SENT:
        got[i] = lax.ppermute(sent[i], RING, along_z(*BLOCKS[i]))
    got[1] = lax.all_gather(sent[1], "c")

    def project(blocks, factor):
        count = len(blocks) * taken
        return call(
            forward_kernel,
            sds((count, 3 * hidden)),
            (*blocks, w_gate, w_up, w_down),
            flops=int(factor * 6 * count * hidden * width),
            scratch=[pltpu.VMEM((count, width), BF16)] * 2,
        )

    def over_x(a):
        return exchange(a.reshape(nx, a.shape[0] // nx, 3 * hidden), "x")

    near = over_x(project([got[i] for i in range(NEAR)], NEAR_COST))
    far = project([got[i] for i in range(NEAR, experts)], FAR_COST)
    far = over_x(call(after_kernel, sds(far.shape), (far, near), flops=0))
    parts = (near, far)
    d_block = call(middle_kernel, sds((block, 2 * hidden + LANES)), parts, flops=30 * block * hidden)
    d = lax.all_gather(d_block, "x", tiled=True)
    part = call(
        functools.partial(backward_kernel, experts),
        sds((ny, rows + PAD, share)),
        (d, w_gate, w_up),
        flops=4 * rows * hidden * width,
    )
    summed = call(
        sum_kernel,
        sds((experts, taken + TAIL, share)),
        (exchange(part, "y"),),
        flops=4 * part.size,
        scratch=[pltpu.VMEM((rows, share), F32)],
    )
    back = exchange(summed, EXPERT)
    mine = call(
        scatter_kernel, sds((tokens + PAD, share)), (picks, scores, back), flops=2 * rows * tokens * share
    )
    over_zh = lax.all_gather(mine, "zh")
    token_grad = call(token_kernel, sds((tokens, share)), (over_zh,), flops=4 * mine.size)
    return call(
        final_kernel,
        (sds((tokens, width)), sds((experts, taken))),
        (lax.all_gather(token_grad, "y"), over_zh),
        flops=0,
    )


def solution(mesh):
    fine = Mesh(mesh.devices.reshape(tuple(SIZES.values())), tuple(SIZES))
    ffn = ("y", "zh")
    placed_in = (
        P(EXPERT, "x"),
        P(EXPERT, "x"),
        P(None, EXPERT),
        P(None, EXPERT),
        P(EXPERT, ffn, "x"),
        P(EXPERT, ffn, "x"),
        P(EXPERT, ffn, "x"),
    )
    return jax.shard_map(
        local,
        mesh=fine,
        in_specs=placed_in,
        out_specs=(P(EXPERT, "x"), P(None, EXPERT)),
        check_vma=False,
    )
```

```python
import functools

import jax
import jax.numpy as jnp
from jax import lax
from jax.experimental import pallas as pl
from jax.experimental.pallas import tpu as pltpu
from jax.sharding import Mesh, PartitionSpec as P

BF16 = jnp.bfloat16
F32 = jnp.float32
LANES = 128
PAD = 16
TAIL = 8
EXPERT = ("zl", "c")
RING = ("zl", "c", "zh")
SIZES = {"zl": 4, "c": 2, "y": 4, "zh": 4, "x": 4}
LIMIT = 16
VMEM = pl.BlockSpec(memory_space=pltpu.VMEM)


def dot(a, b, ca, cb):
    return lax.dot_general(a, b, (((ca,), (cb,)), ((), ())), preferred_element_type=F32)


def iota(shape, axis):
    return lax.broadcasted_iota(jnp.int32, shape, axis)


def sds(shape, dtype=BF16):
    return jax.ShapeDtypeStruct(shape, dtype)


def add_up(pieces):
    return functools.reduce(lambda a, b: a + b, pieces)


def call(kernel, outs, args, *, flops, specs=None, scratch=(), limit=LIMIT):
    nbytes = sum(a.size * a.dtype.itemsize for a in list(args) + jax.tree.leaves(outs))
    return pl.pallas_call(
        kernel,
        out_shape=outs,
        in_specs=specs or [VMEM] * len(args),
        out_specs=jax.tree.map(lambda o: VMEM, outs),
        scratch_shapes=scratch,
        compiler_params=pltpu.CompilerParams(vmem_limit_bytes=limit << 20),
        cost_estimate=pl.CostEstimate(flops=flops, bytes_accessed=nbytes, transcendentals=0),
    )(*args)


BLOCKS = ((0, 0), (0, 1), (1, 0), (-1, 0), (1, 1), (-1, 1), (2, 0), (-2, 1))
NEAR = 6
NEAR_COST, FAR_COST = 1, 10
SENT = (2, 3, 4, 5, 6, 7)


def at(dz, dc):
    chips, cores = SIZES["zl"], SIZES["c"]
    return lax.rem(lax.axis_index("zl") + (dz + chips), chips) * cores + lax.rem(lax.axis_index("c") + dc, cores)


def pick_kernel(picks_ref, xg_ref, *refs):
    *outs, hot_ref = refs
    experts, taken = picks_ref.shape
    tokens, width = xg_ref.shape[1:]
    row = iota(picks_ref.shape, 0)
    values = picks_ref[...].astype(F32)
    picked = [
        jnp.sum(jnp.where(row == at(*b), values, 0.0), axis=0, keepdims=True) for b in BLOCKS
    ]
    picks = jnp.transpose(jnp.concatenate(picked, axis=0))
    lane = iota((taken, tokens), 1).astype(F32)
    for i in range(experts):
        hot_ref[i * taken : (i + 1) * taken, :] = (lane == picks[:, i : i + 1]).astype(BF16)
    step = 4 * LANES
    for which in range(2):
        for start in range(0, width, step):
            cols = slice(start, start + step)
            rows = dot(hot_ref[...], xg_ref[which, :, cols], 1, 0).astype(BF16)
            for i in range(experts):
                outs[i][which, :, cols] = rows[i * taken : (i + 1) * taken]


def after_kernel(a_ref, _, out_ref):
    out_ref[...] = a_ref[...]


def forward_kernel(*refs):
    blocks, (gate_ref, up_ref, down_ref, out_ref, x_ref, g_ref) = refs[:-6], refs[-6:]
    taken = blocks[0].shape[1]
    blocks = [ref if len(ref.shape) == 3 else ref.at[1 - lax.axis_index("c")] for ref in blocks]
    for which, rows_ref in enumerate((x_ref, g_ref)):
        for i, block in enumerate(blocks):
            rows_ref[i * taken : (i + 1) * taken, :] = block[which]
    hidden = gate_ref.shape[0]
    for i, (w_ref, rows_ref) in enumerate(((gate_ref, x_ref), (up_ref, x_ref), (down_ref, g_ref))):
        total = dot(rows_ref[...], w_ref[...], 1, 1)
        out_ref[:, i * hidden : (i + 1) * hidden] = total.astype(BF16)


def middle_kernel(*refs):
    *part_refs, out_ref = refs
    hidden = part_refs[0].shape[2] // 3

    def total(i):
        cols = slice(i * hidden, (i + 1) * hidden)
        sums = [add_up([ref[k, :, cols].astype(F32) for k in range(ref.shape[0])]) for ref in part_refs]
        return jnp.concatenate(sums, axis=0)

    gate, up, back = total(0), total(1), total(2)
    sig = 1.0 / (1.0 + jnp.exp(-gate))
    act = gate * sig
    score = jnp.sum(act * up * back, axis=1, keepdims=True)
    out_ref[:, :hidden] = (back * up * sig * (1.0 + gate * (1.0 - sig))).astype(BF16)
    out_ref[:, hidden : 2 * hidden] = (back * act).astype(BF16)
    high = score.astype(BF16).astype(F32)
    lane = iota((out_ref.shape[0], LANES), 1)
    both = jnp.where(lane == 0, high, jnp.where(lane == 1, score - high, 0.0))
    out_ref[:, 2 * hidden :] = both.astype(BF16)


def in_blocks(row, rows):
    parts = SIZES["x"]
    near = rows * NEAR // len(BLOCKS)
    x, r = row // (rows // parts), row % (rows // parts)
    near_x = near // parts
    return jnp.where(r < near_x, x * near_x + r, near + x * (rows // parts - near_x) + r - near_x)


def score_block(d_scores, shards):
    rows = d_scores.shape[0]
    each = rows // shards
    pick = (iota((PAD, LANES), 0) == iota((PAD, LANES), 1)).astype(BF16)
    lines = dot(pick, d_scores, 1, 1)
    line = iota((PAD, rows), 0)
    block = in_blocks(iota((1, rows), 1), rows) // each
    apart = jnp.where(line == block, lines[0:1, :], jnp.where(line == block + shards, lines[1:2, :], 0.0))
    lane = in_blocks(iota((rows, 1), 0), rows) % each
    return dot(apart.astype(BF16), (iota((rows, LANES), 1) == lane).astype(BF16), 1, 0)


def backward_kernel(shards, d_ref, gate_ref, up_ref, out_ref, w_ref):
    rows, hidden = d_ref.shape[0], gate_ref.shape[0]
    parts, _, share = out_ref.shape
    block = score_block(d_ref[:, 2 * hidden :], shards).astype(BF16)
    for k in range(parts):
        cols = slice(k * share, (k + 1) * share)
        w_ref[k % 2, :hidden, :] = gate_ref[:, cols]
        w_ref[k % 2, hidden:, :] = up_ref[:, cols]
        total = dot(d_ref[:, : 2 * hidden], w_ref[k % 2], 1, 0)
        out_ref[k, :rows, :] = total.astype(BF16)
        out_ref[k, rows:, :] = jnp.zeros((PAD, share), BF16)
        out_ref[k, rows:, :LANES] = block


def sum_kernel(part_ref, out_ref, rows_ref):
    parts, _, share = part_ref.shape
    shards, each, _ = out_ref.shape
    each -= TAIL
    rows = shards * each
    one = rows // SIZES["x"]
    near = one * NEAR // len(BLOCKS)

    def total(start, count):
        return add_up([part_ref[k, start : start + count, :].astype(F32) for k in range(parts)])

    for x in range(SIZES["x"]):
        mine = total(x * one, one)
        rows_ref[x * near : (x + 1) * near, :] = mine[:near]
        far = SIZES["x"] * near + x * (one - near)
        rows_ref[far : far + one - near, :] = mine[near:]
    score = total(rows, PAD)
    score = score[:shards] + score[shards:]
    high = score.astype(BF16).astype(F32)
    low = score - high
    row = iota((TAIL, share), 0)
    for i, (dz, dc) in enumerate(BLOCKS):
        both = jnp.where(row == 0, high[i : i + 1], jnp.where(row == 1, low[i : i + 1], 0.0))
        block = jnp.concatenate([rows_ref[i * each : (i + 1) * each, :], both], axis=0)
        out_ref[at(-dz, dc)] = block.astype(BF16)


def scatter_kernel(picks_ref, weights_ref, back_ref, out_ref):
    experts, taken = picks_ref.shape
    tokens, share = out_ref.shape[0] - PAD, out_ref.shape[1]
    weights = weights_ref[...].astype(F32)
    scores = jnp.zeros((PAD, share), F32)
    line = iota((PAD, share), 0)
    token = iota((tokens, taken), 0)
    terms = []
    for e in range(experts):
        block = back_ref[e].astype(F32)
        lines = block[taken:]
        scores = jnp.where(line == e, lines[0:1], jnp.where(line == e + experts, lines[1:2], scores))
        placed = jnp.where(token == picks_ref[e : e + 1, :], weights[e : e + 1, :], 0.0).astype(BF16)
        terms.append(dot(placed, block[:taken].astype(BF16), 1, 0))
    out_ref[:tokens, :] = add_up(terms).astype(BF16)
    out_ref[tokens:, :] = scores.astype(BF16)


def token_kernel(part_ref, out_ref):
    tokens = out_ref.shape[0]
    out_ref[...] = add_up([part_ref[k, :tokens, :].astype(F32) for k in range(part_ref.shape[0])]).astype(BF16)


def final_kernel(gathered_ref, part_ref, grad_ref, score_ref):
    parts, tokens, share = gathered_ref.shape
    experts, taken = score_ref.shape
    for k in range(parts):
        grad_ref[:, k * share : (k + 1) * share] = gathered_ref[k]
    total = add_up([part_ref[k, tokens:, :].astype(F32) for k in range(part_ref.shape[0])])
    score = total[:experts] + total[experts:]
    score_ref[...] = score[:, :taken].astype(BF16)


def exchange(a, axes):
    return lax.all_to_all(a, axes, split_axis=0, concat_axis=0, tiled=True)


def along_z(dz, dc):
    nl, nc, nh = (SIZES[a] for a in RING)
    return [
        ((z % nl * nc + c) * nh + z // nl, (to % nl * nc + (c + dc) % nc) * nh + to // nl)
        for z in range(nl * nh)
        for to in [(z + dz) % (nl * nh)]
        for c in range(nc)
    ]


def local(layer_input, out_grad, scores, picks, w_gate, w_up, w_down):
    experts, taken = picks.shape
    tokens, width = layer_input.shape
    w_gate, w_up, w_down = w_gate[0], w_up[0], w_down[0]
    hidden = w_gate.shape[0]
    rows = experts * taken
    ny, nx = SIZES["y"], SIZES["x"]
    share, block = width // ny, rows // nx

    sent = call(
        pick_kernel,
        [sds((2, taken, width))] * experts,
        (picks, jnp.concatenate([layer_input, out_grad]).reshape(2, tokens, width)),
        flops=4 * rows * tokens * width,
        scratch=[pltpu.VMEM((rows, tokens), BF16)],
    )
    got = {0: sent[0]}
    for i in SENT:
        got[i] = lax.ppermute(sent[i], RING, along_z(*BLOCKS[i]))
    got[1] = lax.all_gather(sent[1], "c")

    def project(blocks, factor):
        count = len(blocks) * taken
        return call(
            forward_kernel,
            sds((count, 3 * hidden)),
            (*blocks, w_gate, w_up, w_down),
            flops=int(factor * 6 * count * hidden * width),
            scratch=[pltpu.VMEM((count, width), BF16)] * 2,
        )

    def over_x(a):
        return exchange(a.reshape(nx, a.shape[0] // nx, 3 * hidden), "x")

    near = over_x(project([got[i] for i in range(NEAR)], NEAR_COST))
    far = project([got[i] for i in range(NEAR, experts)], FAR_COST)
    far = over_x(call(after_kernel, sds(far.shape), (far, near), flops=0))
    parts = (near, far)
    d_block = call(middle_kernel, sds((block, 2 * hidden + LANES)), parts, flops=30 * block * hidden)
    d = lax.all_gather(d_block, "x", tiled=True)
    part = call(
        functools.partial(backward_kernel, experts),
        sds((ny, rows + PAD, share)),
        (d, w_gate, w_up),
        flops=4 * rows * hidden * width,
        scratch=[pltpu.VMEM((2, 2 * hidden, share), BF16)],
    )
    summed = call(
        sum_kernel,
        sds((experts, taken + TAIL, share)),
        (exchange(part, "y"),),
        flops=4 * part.size,
        scratch=[pltpu.VMEM((rows, share), F32)],
    )
    back = exchange(summed, EXPERT)
    mine = call(
        scatter_kernel, sds((tokens + PAD, share)), (picks, scores, back), flops=2 * rows * tokens * share
    )
    over_zh = lax.all_gather(mine, "zh")
    token_grad = call(token_kernel, sds((tokens, share)), (over_zh,), flops=4 * mine.size)
    return call(
        final_kernel,
        (sds((tokens, width)), sds((experts, taken))),
        (lax.all_gather(token_grad, "y"), over_zh),
        flops=0,
    )


def solution(mesh):
    fine = Mesh(mesh.devices.reshape(tuple(SIZES.values())), tuple(SIZES))
    ffn = ("y", "zh")
    placed_in = (
        P(EXPERT, "x"),
        P(EXPERT, "x"),
        P(None, EXPERT),
        P(None, EXPERT),
        P(EXPERT, ffn, "x"),
        P(EXPERT, ffn, "x"),
        P(EXPERT, ffn, "x"),
    )
    return jax.shard_map(
        local,
        mesh=fine,
        in_specs=placed_in,
        out_specs=(P(EXPERT, "x"), P(None, EXPERT)),
        check_vma=False,
    )
```

```python
import functools

import jax
import jax.numpy as jnp
from jax import lax
from jax.experimental import pallas as pl
from jax.experimental.pallas import tpu as pltpu
from jax.sharding import Mesh, PartitionSpec as P

BF16 = jnp.bfloat16
F32 = jnp.float32
LANES = 128
PAD = 16
TAIL = 8
EXPERT = ("zl", "c")
RING = ("zl", "c", "zh")
SIZES = {"zl": 4, "c": 2, "y": 4, "zh": 4, "x": 4}
LIMIT = 16
VMEM = pl.BlockSpec(memory_space=pltpu.VMEM)


def dot(a, b, ca, cb):
    return lax.dot_general(a, b, (((ca,), (cb,)), ((), ())), preferred_element_type=F32)


def iota(shape, axis):
    return lax.broadcasted_iota(jnp.int32, shape, axis)


def sds(shape, dtype=BF16):
    return jax.ShapeDtypeStruct(shape, dtype)


def add_up(pieces):
    return functools.reduce(lambda a, b: a + b, pieces)


def call(kernel, outs, args, *, flops, specs=None, scratch=(), limit=LIMIT):
    nbytes = sum(a.size * a.dtype.itemsize for a in list(args) + jax.tree.leaves(outs))
    return pl.pallas_call(
        kernel,
        out_shape=outs,
        in_specs=specs or [VMEM] * len(args),
        out_specs=jax.tree.map(lambda o: VMEM, outs),
        scratch_shapes=scratch,
        compiler_params=pltpu.CompilerParams(vmem_limit_bytes=limit << 20),
        cost_estimate=pl.CostEstimate(flops=flops, bytes_accessed=nbytes, transcendentals=0),
    )(*args)


BLOCKS = ((0, 0), (0, 1), (1, 0), (-1, 0), (1, 1), (-1, 1), (2, 0), (-2, 1))
NEAR = 6
NEAR_COST, FAR_COST = 1, 10
SENT = (2, 3, 4, 5, 6, 7)


def at(dz, dc):
    chips, cores = SIZES["zl"], SIZES["c"]
    return lax.rem(lax.axis_index("zl") + (dz + chips), chips) * cores + lax.rem(lax.axis_index("c") + dc, cores)


def pick_kernel(picks_ref, xg_ref, *refs):
    *outs, hot_ref = refs
    experts, taken = picks_ref.shape
    tokens, width = xg_ref.shape[1:]
    row = iota(picks_ref.shape, 0)
    values = picks_ref[...].astype(F32)
    picked = [
        jnp.sum(jnp.where(row == at(*b), values, 0.0), axis=0, keepdims=True) for b in BLOCKS
    ]
    picks = jnp.transpose(jnp.concatenate(picked, axis=0))
    lane = iota((taken, tokens), 1).astype(F32)
    for i in range(experts):
        hot_ref[i * taken : (i + 1) * taken, :] = (lane == picks[:, i : i + 1]).astype(BF16)
    step = 4 * LANES
    for which in range(2):
        for start in range(0, width, step):
            cols = slice(start, start + step)
            rows = dot(hot_ref[...], xg_ref[which, :, cols], 1, 0).astype(BF16)
            for i in range(experts):
                outs[i][which, :, cols] = rows[i * taken : (i + 1) * taken]


def after_kernel(a_ref, _, out_ref):
    out_ref[...] = a_ref[...]


def forward_kernel(*refs):
    blocks, (gate_ref, up_ref, down_ref, out_ref, x_ref, g_ref) = refs[:-6], refs[-6:]
    taken = blocks[0].shape[1]
    blocks = [ref if len(ref.shape) == 3 else ref.at[1 - lax.axis_index("c")] for ref in blocks]
    for which, rows_ref in enumerate((x_ref, g_ref)):
        for i, block in enumerate(blocks):
            rows_ref[i * taken : (i + 1) * taken, :] = block[which]
    hidden = gate_ref.shape[0]
    for i, (w_ref, rows_ref) in enumerate(((gate_ref, x_ref), (up_ref, x_ref), (down_ref, g_ref))):
        total = dot(rows_ref[...], w_ref[...], 1, 1)
        out_ref[:, i * hidden : (i + 1) * hidden] = total.astype(BF16)


def middle_kernel(*refs):
    *part_refs, out_ref = refs
    hidden = part_refs[0].shape[2] // 3

    def total(i):
        cols = slice(i * hidden, (i + 1) * hidden)
        sums = [add_up([ref[k, :, cols].astype(F32) for k in range(ref.shape[0])]) for ref in part_refs]
        return jnp.concatenate(sums, axis=0)

    gate, up, back = total(0), total(1), total(2)
    sig = 1.0 / (1.0 + jnp.exp(-gate))
    act = gate * sig
    score = jnp.sum(act * up * back, axis=1, keepdims=True)
    out_ref[:, :hidden] = (back * up * sig * (1.0 + gate * (1.0 - sig))).astype(BF16)
    out_ref[:, hidden : 2 * hidden] = (back * act).astype(BF16)
    high = score.astype(BF16).astype(F32)
    lane = iota((out_ref.shape[0], LANES), 1)
    both = jnp.where(lane == 0, high, jnp.where(lane == 1, score - high, 0.0))
    out_ref[:, 2 * hidden :] = both.astype(BF16)


def in_blocks(row, rows):
    parts = SIZES["x"]
    near = rows * NEAR // len(BLOCKS)
    x, r = row // (rows // parts), row % (rows // parts)
    near_x = near // parts
    return jnp.where(r < near_x, x * near_x + r, near + x * (rows // parts - near_x) + r - near_x)


def score_block(d_scores, shards):
    rows = d_scores.shape[0]
    each = rows // shards
    block = in_blocks(iota((1, rows), 1), rows) // each
    own = (iota((PAD, rows), 0) == block).astype(BF16)
    here = iota((rows, LANES), 1) == in_blocks(iota((rows, 1), 0), rows) % each
    values = d_scores.astype(F32)
    high, low = (jnp.where(here, values[:, i : i + 1], 0.0).astype(BF16) for i in range(2))
    both = dot(own, jnp.concatenate([high, low], axis=1), 1, 0)
    return jnp.concatenate([both[:shards, :LANES], both[:shards, LANES:]], axis=0)


def backward_kernel(shards, d_ref, gate_ref, up_ref, out_ref, w_ref):
    rows, hidden = d_ref.shape[0], gate_ref.shape[0]
    parts, _, share = out_ref.shape
    block = score_block(d_ref[:, 2 * hidden :], shards).astype(BF16)
    for k in range(parts):
        cols = slice(k * share, (k + 1) * share)
        w_ref[k % 2, :hidden, :] = gate_ref[:, cols]
        w_ref[k % 2, hidden:, :] = up_ref[:, cols]
        total = dot(d_ref[:, : 2 * hidden], w_ref[k % 2], 1, 0)
        out_ref[k, :rows, :] = total.astype(BF16)
        out_ref[k, rows:, :] = jnp.zeros((PAD, share), BF16)
        out_ref[k, rows:, :LANES] = block


def sum_kernel(part_ref, out_ref, rows_ref):
    parts, _, share = part_ref.shape
    shards, each, _ = out_ref.shape
    each -= TAIL
    rows = shards * each
    one = rows // SIZES["x"]
    near = one * NEAR // len(BLOCKS)

    def total(start, count):
        return add_up([part_ref[k, start : start + count, :].astype(F32) for k in range(parts)])

    for x in range(SIZES["x"]):
        mine = total(x * one, one)
        rows_ref[x * near : (x + 1) * near, :] = mine[:near]
        far = SIZES["x"] * near + x * (one - near)
        rows_ref[far : far + one - near, :] = mine[near:]
    score = total(rows, PAD)
    score = score[:shards] + score[shards:]
    high = score.astype(BF16).astype(F32)
    low = score - high
    row = iota((TAIL, share), 0)
    for i, (dz, dc) in enumerate(BLOCKS):
        both = jnp.where(row == 0, high[i : i + 1], jnp.where(row == 1, low[i : i + 1], 0.0))
        block = jnp.concatenate([rows_ref[i * each : (i + 1) * each, :], both], axis=0)
        out_ref[at(-dz, dc)] = block.astype(BF16)


def scatter_kernel(picks_ref, weights_ref, back_ref, out_ref):
    experts, taken = picks_ref.shape
    tokens, share = out_ref.shape[0] - PAD, out_ref.shape[1]
    weights = weights_ref[...].astype(F32)
    scores = jnp.zeros((PAD, share), F32)
    line = iota((PAD, share), 0)
    token = iota((tokens, taken), 0)
    terms = []
    for e in range(experts):
        block = back_ref[e].astype(F32)
        lines = block[taken:]
        scores = jnp.where(line == e, lines[0:1], jnp.where(line == e + experts, lines[1:2], scores))
        placed = jnp.where(token == picks_ref[e : e + 1, :], weights[e : e + 1, :], 0.0).astype(BF16)
        terms.append(dot(placed, block[:taken].astype(BF16), 1, 0))
    out_ref[:tokens, :] = add_up(terms).astype(BF16)
    out_ref[tokens:, :] = scores.astype(BF16)


def token_kernel(part_ref, out_ref):
    tokens = out_ref.shape[0]
    out_ref[...] = add_up([part_ref[k, :tokens, :].astype(F32) for k in range(part_ref.shape[0])]).astype(BF16)


def final_kernel(gathered_ref, part_ref, grad_ref, score_ref):
    parts, tokens, share = gathered_ref.shape
    experts, taken = score_ref.shape
    for k in range(parts):
        grad_ref[:, k * share : (k + 1) * share] = gathered_ref[k]
    total = add_up([part_ref[k, tokens:, :].astype(F32) for k in range(part_ref.shape[0])])
    score = total[:experts] + total[experts:]
    score_ref[...] = score[:, :taken].astype(BF16)


def exchange(a, axes):
    return lax.all_to_all(a, axes, split_axis=0, concat_axis=0, tiled=True)


def along_z(dz, dc):
    nl, nc, nh = (SIZES[a] for a in RING)
    return [
        ((z % nl * nc + c) * nh + z // nl, (to % nl * nc + (c + dc) % nc) * nh + to // nl)
        for z in range(nl * nh)
        for to in [(z + dz) % (nl * nh)]
        for c in range(nc)
    ]


def local(layer_input, out_grad, scores, picks, w_gate, w_up, w_down):
    experts, taken = picks.shape
    tokens, width = layer_input.shape
    w_gate, w_up, w_down = w_gate[0], w_up[0], w_down[0]
    hidden = w_gate.shape[0]
    rows = experts * taken
    ny, nx = SIZES["y"], SIZES["x"]
    share, block = width // ny, rows // nx

    sent = call(
        pick_kernel,
        [sds((2, taken, width))] * experts,
        (picks, jnp.concatenate([layer_input, out_grad]).reshape(2, tokens, width)),
        flops=4 * rows * tokens * width,
        scratch=[pltpu.VMEM((rows, tokens), BF16)],
    )
    got = {0: sent[0]}
    for i in SENT:
        got[i] = lax.ppermute(sent[i], RING, along_z(*BLOCKS[i]))
    got[1] = lax.all_gather(sent[1], "c")

    def project(blocks, factor):
        count = len(blocks) * taken
        return call(
            forward_kernel,
            sds((count, 3 * hidden)),
            (*blocks, w_gate, w_up, w_down),
            flops=int(factor * 6 * count * hidden * width),
            scratch=[pltpu.VMEM((count, width), BF16)] * 2,
        )

    def over_x(a):
        return exchange(a.reshape(nx, a.shape[0] // nx, 3 * hidden), "x")

    near = over_x(project([got[i] for i in range(NEAR)], NEAR_COST))
    far = project([got[i] for i in range(NEAR, experts)], FAR_COST)
    far = over_x(call(after_kernel, sds(far.shape), (far, near), flops=0))
    parts = (near, far)
    d_block = call(middle_kernel, sds((block, 2 * hidden + LANES)), parts, flops=30 * block * hidden)
    d = lax.all_gather(d_block, "x", tiled=True)
    part = call(
        functools.partial(backward_kernel, experts),
        sds((ny, rows + PAD, share)),
        (d, w_gate, w_up),
        flops=4 * rows * hidden * width,
        scratch=[pltpu.VMEM((2, 2 * hidden, share), BF16)],
    )
    summed = call(
        sum_kernel,
        sds((experts, taken + TAIL, share)),
        (exchange(part, "y"),),
        flops=4 * part.size,
        scratch=[pltpu.VMEM((rows, share), F32)],
    )
    back = exchange(summed, EXPERT)
    mine = call(
        scatter_kernel, sds((tokens + PAD, share)), (picks, scores, back), flops=2 * rows * tokens * share
    )
    over_zh = lax.all_gather(mine, "zh")
    token_grad = call(token_kernel, sds((tokens, share)), (over_zh,), flops=4 * mine.size)
    return call(
        final_kernel,
        (sds((tokens, width)), sds((experts, taken))),
        (lax.all_gather(token_grad, "y"), over_zh),
        flops=0,
    )


def solution(mesh):
    fine = Mesh(mesh.devices.reshape(tuple(SIZES.values())), tuple(SIZES))
    ffn = ("y", "zh")
    placed_in = (
        P(EXPERT, "x"),
        P(EXPERT, "x"),
        P(None, EXPERT),
        P(None, EXPERT),
        P(EXPERT, ffn, "x"),
        P(EXPERT, ffn, "x"),
        P(EXPERT, ffn, "x"),
    )
    return jax.shard_map(
        local,
        mesh=fine,
        in_specs=placed_in,
        out_specs=(P(EXPERT, "x"), P(None, EXPERT)),
        check_vma=False,
    )
```
